256 devices in a mesh: row: 16 (over z, y_lo), col: 8 (over x, core), rep: 2 (over y_hi).
Axes of the slice: x: 4, y: 4 (y_hi: 2, y_lo: 2; y = y_hi * 2 + y_lo), z: 8, core: 2. Of those that a mesh axis runs over, the one named last changes fastest.
Arguments:
- a_blocks: bfloat16 [128, 16, 2, 128, 128], P('row', 'col'), may hold values from -0.25 to 0.25
- a_index: int32 [128, 16, 2], P('row', 'col'), may hold values from 0 to 63, as said below
- a_count: int32 [128, 16], P('row', 'col'), may hold values from 0 to 2, as said below
- b_blocks: bfloat16 [16, 8, 32, 128, 128], P('row', 'col'), may hold values from -6 to 6
- b_rows: int32 [16, 8, 32], P('row', 'col'), may hold values from 0 to 63, as said below
- b_cols: int32 [16, 8, 32], P('row', 'col'), may hold values from 0 to 63
- b_count: int32 [16, 8], P('row', 'col'), may hold values from 16 to 32, as said below
- c_cols: int32 [128, 8, 4], P('row', 'col'), may hold values from 0 to 63, as said below
- c_count: int32 [128, 8], P('row', 'col'), may hold values from 1 to 4, as said below
Outputs:
- c_blocks: bfloat16 [128, 8, 4, 128, 128], P(('row', 'rep'), 'col')
The draws below stay inside these ranges and needn't reach their ends.
Inputs may be any that keep to these rules, and one draw needn't show every extreme that they name: Live slots come first: slot a of block row i in piece p is live when a < a_count[i, p]. `a_index`: the slots of one block row and piece name distinct block rows of that piece. Live slots come first: slot m of list (p, q) is live when m < b_count[p, q]. `b_rows`: the slots of one list name distinct block rows of the piece. Live slots come first: slot s of block row i in group q is live when s < c_count[i, q]. `c_cols`: the slots of one block row and group name distinct block columns.
All inputs are finite; a program needn't handle non-finite values.
Results may differ from the reference program's by a relative error of at most 0.001.
Values may be sent and summed in bfloat16 or wider, within the bound.
No kernel may reach another device: no remote copies, remote signals or barrier semaphores. Data moves between devices by JAX's collectives and lax.ppermute only.
A program may use at most 64 MiB of HBM per device.

```python
import jax
import jax.numpy as jnp
from jax import lax

BS = 128
SA = 2
MB = 32
SC = 4
KP = 16
INNER_BLOCKS = 64
CG = 8
CB = 64
NBR = 128


def solute_rows(key):
    key = jax.random.fold_in(key, 101)
    solute_start = jax.random.randint(key, (), 0, NBR)
    row_ids = jnp.arange(NBR, dtype=jnp.int32)
    inside = (row_ids - solute_start) % NBR < max(NBR // 8, 1)
    return (solute_start, inside)


def window_width():
    return min(SC + 2, CB)


def group_offsets(key):
    key = jax.random.fold_in(key, 404)
    width = window_width()
    offsets = jax.random.randint(key, (CG,), 0, CB - width + 1)
    group_ids = jnp.arange(CG, dtype=jnp.int32)
    offsets = jnp.where(group_ids == 0, CB - width, offsets)
    offsets = jnp.where(group_ids == 1, 0, offsets)
    return offsets.astype(jnp.int32)


def b_row_lists(key):
    key = jax.random.fold_in(key, 202)
    ranking_values = jax.random.randint(key, (KP, CG, INNER_BLOCKS), 0, 1 << 20) * INNER_BLOCKS + jnp.arange(INNER_BLOCKS, dtype=jnp.int32)
    return jnp.argsort(ranking_values, axis=-1)[:, :, :MB].astype(jnp.int32)


def c_counts(key):
    solute_start, inside = solute_rows(key)
    key = jax.random.fold_in(key, 303)
    counts = jax.random.randint(key, (NBR, CG), 1, SC + 1)
    return jnp.where(inside[:, None], SC, counts).astype(jnp.int32)


def draw_a_index(key, part):
    key = jax.random.fold_in(key, 1)
    ranking_values = jax.random.randint(key, (NBR, KP, INNER_BLOCKS), 0, 1 << 20) * INNER_BLOCKS + jnp.arange(INNER_BLOCKS, dtype=jnp.int32)
    row_ids = jnp.arange(NBR, dtype=jnp.int32)[:, None, None]
    piece_ids = jnp.arange(KP, dtype=jnp.int32)[None, :, None]
    inner_ids = jnp.arange(INNER_BLOCKS, dtype=jnp.int32)[None, None, :]
    extra_credit = (1 << 20) * INNER_BLOCKS * 2
    upper_bound_position = (row_ids == 0) & (piece_ids == 0) & (inner_ids == INNER_BLOCKS - 1)
    lower_bound_position = (row_ids == 0) & (piece_ids == 1) & (inner_ids == 0)
    ranking_values = jnp.where(upper_bound_position | lower_bound_position, ranking_values + extra_credit, ranking_values)
    return jnp.argsort(-ranking_values, axis=-1)[:, :, :SA].astype(jnp.int32)


def draw_a_count(key, part):
    solute_start, inside = solute_rows(key)
    key = jax.random.fold_in(key, 2)
    counts = jax.random.randint(key, (NBR, KP), 0, SA + 1)
    counts = jnp.where(inside[:, None], SA, counts)
    empty_row = (solute_start + NBR // 2) % NBR
    row_ids = jnp.arange(NBR, dtype=jnp.int32)[:, None]
    piece_ids = jnp.arange(KP, dtype=jnp.int32)[None, :]
    counts = jnp.where((row_ids == empty_row) & (piece_ids == 0), 0, counts)
    return counts.astype(jnp.int32)


def draw_b_count(key, part):
    key = jax.random.fold_in(key, 3)
    key_count, key_full = jax.random.split(key)
    counts = jax.random.randint(key_count, (KP, CG), MB // 2, MB + 1)
    full_at = jax.random.randint(key_full, (), 0, KP * CG)
    flat = jnp.where(jnp.arange(KP * CG, dtype=jnp.int32) == full_at, MB, counts.reshape(-1))
    return flat.reshape(KP, CG).astype(jnp.int32)


def draw_b_rows(key, part):
    lists = b_row_lists(key)
    return lists


def draw_b_cols(key, part):
    offsets = group_offsets(key)
    key = jax.random.fold_in(key, 5)
    width = window_width()
    within = jax.random.randint(key, (KP, CG, MB), 0, width)
    piece_ids = jnp.arange(KP, dtype=jnp.int32)[:, None, None]
    group_ids = jnp.arange(CG, dtype=jnp.int32)[None, :, None]
    slot_ids = jnp.arange(MB, dtype=jnp.int32)[None, None, :]
    first = (piece_ids == 0) & (slot_ids == 0)
    within = jnp.where(first & (group_ids == 0), width - 1, within)
    within = jnp.where(first & (group_ids == 1), 0, within)
    return (offsets[None, :, None] + within).astype(jnp.int32)


def draw_c_count(key, part):
    counts = c_counts(key)
    return counts


def draw_c_cols(key, part):
    offsets = group_offsets(key)
    key = jax.random.fold_in(key, 7)
    width = window_width()
    start = jax.random.randint(key, (NBR, CG), 0, width - SC + 1)
    row_ids = jnp.arange(NBR, dtype=jnp.int32)[:, None]
    group_ids = jnp.arange(CG, dtype=jnp.int32)[None, :]
    start = jnp.where((row_ids == 0) & (group_ids == 0), width - SC, start)
    start = jnp.where((row_ids == 0) & (group_ids == 1), 0, start)
    first_col = offsets[None, :] + start
    return (first_col[:, :, None] + jnp.arange(SC, dtype=jnp.int32)[None, None, :]).astype(jnp.int32)


def levels(key, shape, pieces, low, largest):
    gain, own = 1.0, jax.random.fold_in(key, 6)
    for dim, parts in pieces:
        heights = jnp.exp(jax.random.uniform(jax.random.fold_in(own, dim), (parts,), jnp.float32, low / len(pieces), largest / len(pieces)))
        gain = gain * jnp.repeat(heights, shape[dim] // parts).reshape([-1 if axis == dim else 1 for axis in range(len(shape))])
    return gain


def normal_values(rng, shape, spread, reach, shards=(), kind=jnp.bfloat16):
    loudness = levels(rng, shape, shards, -0.22, 0.18) if shards else 1.0
    entries = jax.random.normal(rng, shape, jnp.float32) * spread * loudness
    return jnp.minimum(jnp.maximum(entries, -reach), reach).astype(kind)


def setup_inputs(seed: int = 0) -> dict:
    arg_keys = jax.random.split(jax.random.key(seed), 10)
    return {
        "a_blocks": normal_values(arg_keys[0], (NBR, KP, SA, BS, BS), (4 * BS) ** -0.5, 0.25, ((0, 16), (1, 8))),
        "a_index": draw_a_index(jax.random.fold_in(arg_keys[9], 71), 0),
        "a_count": draw_a_count(jax.random.fold_in(arg_keys[9], 71), 0),
        "b_blocks": normal_values(arg_keys[3], (KP, CG, MB, BS, BS), 1.0, 6.0, ((0, 16), (1, 8))),
        "b_rows": draw_b_rows(jax.random.fold_in(arg_keys[9], 71), 0),
        "b_cols": draw_b_cols(jax.random.fold_in(arg_keys[9], 71), 0),
        "b_count": draw_b_count(jax.random.fold_in(arg_keys[9], 71), 0),
        "c_cols": draw_c_cols(jax.random.fold_in(arg_keys[9], 71), 0),
        "c_count": draw_c_count(jax.random.fold_in(arg_keys[9], 71), 0),
    }


def reference(a_blocks, a_index, a_count, b_blocks, b_rows, b_cols, b_count, c_cols, c_count):
    slots_a = jnp.arange(SA, dtype=jnp.int32)
    slots_b = jnp.arange(MB, dtype=jnp.int32)
    slots_c = jnp.arange(SC, dtype=jnp.int32)
    group_ids = jnp.arange(CG, dtype=jnp.int32)
    a_live = slots_a[None, None, :] < a_count[:, :, None]
    b_live = slots_b[None, None, :] < b_count[:, :, None]
    c_live = slots_c[None, None, :] < c_count[:, :, None]

    def add_piece(running, piece_no):
        k_index = a_index[:, piece_no]
        b_row_list = b_rows[piece_no]
        matches = (k_index[:, :, None, None] == b_row_list[None, None, :, :]) & b_live[piece_no][None, None, :, :] & a_live[:, piece_no][:, :, None, None]
        b_slot = jnp.sum(jnp.where(matches, slots_b, jnp.int32(0)), axis=-1).astype(jnp.int32)
        found_position = jnp.any(matches, axis=-1)
        picked = b_blocks[piece_no][group_ids[None, None, :], b_slot]
        target = b_cols[piece_no][group_ids[None, None, :], b_slot]
        landing = (c_cols[:, None, :, :] == target[:, :, :, None]) & found_position[:, :, :, None] & c_live[:, None, :, :]
        products = jnp.einsum("iaxy,iaqyz->iaqxz", a_blocks[:, piece_no].astype(jnp.float32), picked.astype(jnp.float32), precision=lax.Precision.HIGHEST)
        running = running + jnp.einsum("iaqs,iaqxz->iqsxz", landing.astype(jnp.float32), products, precision=lax.Precision.HIGHEST)
        return running, None

    initial = jnp.zeros((NBR, CG, SC, BS, BS), jnp.float32)
    running, _ = lax.scan(add_piece, initial, jnp.arange(KP, dtype=jnp.int32))
    return running.astype(jnp.bfloat16)
```

```python
import functools

import jax
import jax.numpy as jnp
from jax import lax
from jax.experimental import pallas as pl
from jax.experimental.pallas import tpu as pltpu
from jax.sharding import Mesh
from jax.sharding import PartitionSpec as P

NZ, NYL, NX, NCORE, NREP = 8, 2, 4, 2, 2
AXES = ("z", "yl", "x", "core", "rep")
COL = ("x", "core")
BS, SA, SC, MB = 128, 2, 4, 32
ROWS = 4
PAIR = ROWS * 2 * SA
CAP = 10
HDR = 16
LANES = 128


def y_index(y):
    return (y % NYL) * NREP + y // NYL


def shift_y(value, steps):
    n = NYL * NREP
    return lax.ppermute(value, ("yl", "rep"), [(y_index(y), y_index((y + steps) % n)) for y in range(n)])


def spread(value, axis_name):
    return lax.all_to_all(value, axis_name, 0, 0)


def pack_kernel(lo, size, meta, own, other, b_own, b_low, b_high, out, held, codes, scalars, sems):
    copies = [
        pltpu.make_async_copy(b_own, held.at[pl.ds(0, MB)], sems.at[0]),
        pltpu.make_async_copy(b_low, held.at[pl.ds(MB, MB // 2)], sems.at[1]),
        pltpu.make_async_copy(b_high, held.at[pl.ds(MB + MB // 2, MB // 2)], sems.at[2]),
    ]
    for copy in copies:
        copy.start()
    yl = lax.axis_index("yl")
    lane = lax.broadcasted_iota(jnp.int32, (NZ, LANES), 1)
    is_own = ((lane >> 1) & 1) == yl
    wanted = meta[:, :LANES]
    slot = jnp.zeros((NZ, LANES), jnp.int32)
    target = jnp.full((NZ, LANES), -5, jnp.int32)
    for m in range(MB):
        hit = wanted == jnp.where(is_own, own[0, m], other[0, m])
        slot = jnp.where(hit, m, slot)
        target = jnp.where(hit, jnp.where(is_own, own[1, m], other[1, m]), target)
    code = jnp.full((NZ, LANES), -1, jnp.int32)
    for s in range(SC):
        code = jnp.where(meta[:, (s + 1) * LANES : (s + 2) * LANES] == target, slot * SC + s, code)
    codes[...] = code
    to_scalars = pltpu.make_async_copy(codes, scalars, sems.at[3])
    to_scalars.start()
    head = jnp.concatenate([code, jnp.full((HDR - NZ, LANES), -1, jnp.int32)], axis=0)
    head = head.astype(jnp.float32).astype(jnp.bfloat16)
    for z in range(NZ):
        out[z, pl.ds(size * BS, HDR), :] = head
    to_scalars.wait()
    for copy in copies:
        copy.wait()

    def per_z(z, carry):
        def step(t, count):
            code = scalars[z, t]
            hit = code >= 0

            @pl.when(hit & (count >= lo) & (count < lo + size))
            def _():
                block = (code >> 2) + jnp.where(((t >> 1) & 1) == yl, 0, MB)
                out[z, pl.ds(pl.multiple_of((count - lo) * BS, BS), BS), :] = held[block]

            return count + hit.astype(jnp.int32)

        lax.fori_loop(0, PAIR, step, jnp.int32(0))
        return carry

    lax.fori_loop(0, NZ, per_z, 0)


def pack(meta, own, other, b_own, b_low, b_high, lo, size):
    smem, vmem, hbm = (pl.BlockSpec(memory_space=m) for m in (pltpu.SMEM, pltpu.VMEM, pl.ANY))
    return pl.pallas_call(
        functools.partial(pack_kernel, lo, size),
        out_shape=jax.ShapeDtypeStruct((NZ, size * BS + HDR, BS), jnp.bfloat16),
        in_specs=[vmem, smem, smem, hbm, hbm, hbm],
        out_specs=vmem,
        scratch_shapes=[
            pltpu.VMEM((2 * MB, BS, BS), jnp.bfloat16),
            pltpu.VMEM((NZ, LANES), jnp.int32),
            pltpu.SMEM((NZ, LANES), jnp.int32),
            pltpu.SemaphoreType.DMA((4,)),
        ],
        compiler_params=pltpu.CompilerParams(vmem_limit_bytes=24 * 2**20),
        name="pack",
    )(meta, own, other, b_own, b_low, b_high)


def consume_kernel(parts, a_all, *rest):
    msgs, (out, longest, total, codes, scalars, sem) = rest[: len(parts)], rest[len(parts) :]
    me = lax.axis_index("z")
    row = lax.broadcasted_iota(jnp.int32, (HDR, LANES), 0)
    most = jnp.zeros((HDR, 1), jnp.int32)
    for z in range(NZ):
        head = msgs[0][z, pl.ds(parts[0][1] * BS, HDR), :].astype(jnp.float32).astype(jnp.int32)
        codes[pl.ds(z, 1), :] = jnp.sum(jnp.where(row == me, head, 0), axis=0, keepdims=True)
        most = jnp.maximum(most, jnp.sum((head >= 0).astype(jnp.int32), axis=1, keepdims=True))
    to_scalars = pltpu.make_async_copy(codes, scalars, sem)
    to_scalars.start()
    longest[...] = jnp.broadcast_to(jnp.max(most, axis=0, keepdims=True), longest.shape)
    total[...] = jnp.zeros_like(total)
    to_scalars.wait()

    def per_z(z, carry):
        def step(t, count):
            code = scalars[z, t]
            hit = code >= 0
            place = (t >> 2) * SC + (code & 3)
            for (lo, size), msg in zip(parts, msgs):

                @pl.when(hit & (count >= lo) & (count < lo + size))
                def _(lo=lo, msg=msg):
                    block = msg[z, pl.ds(pl.multiple_of((count - lo) * BS, BS), BS), :]
                    total[place] += jnp.dot(a_all[z, t], block, preferred_element_type=jnp.float32)

            return count + hit.astype(jnp.int32)

        lax.fori_loop(0, PAIR, step, jnp.int32(0))
        return carry

    lax.fori_loop(0, NZ, per_z, 0)
    out[...] = total[...].astype(out.dtype)


def consume(a_all, msgs, parts):
    vmem = pl.BlockSpec(memory_space=pltpu.VMEM)
    return pl.pallas_call(
        functools.partial(consume_kernel, parts),
        out_shape=(
            jax.ShapeDtypeStruct((ROWS * SC, BS, BS), jnp.bfloat16),
            jax.ShapeDtypeStruct((8, LANES), jnp.int32),
        ),
        in_specs=[vmem] * (1 + len(msgs)),
        out_specs=(vmem, vmem),
        scratch_shapes=[
            pltpu.VMEM((ROWS * SC, BS, BS), jnp.float32),
            pltpu.VMEM((NZ, LANES), jnp.int32),
            pltpu.SMEM((NZ, LANES), jnp.int32),
            pltpu.SemaphoreType.DMA,
        ],
        compiler_params=pltpu.CompilerParams(vmem_limit_bytes=24 * 2**20),
        name="consume",
    )(a_all, *msgs)


def body(a_blocks, a_index, a_count, b_blocks, b_rows, b_cols, b_count, c_cols, c_count):
    rep = lax.axis_index("rep")

    def half(value, dim):
        return lax.dynamic_slice_in_dim(value, rep * ROWS, ROWS, dim)

    slots_b = jnp.arange(MB, dtype=jnp.int32)
    own = jnp.stack([jnp.where(slots_b < b_count[0, 0], b_rows[0, 0], -1), b_cols[0, 0]])
    slots_a = jnp.arange(SA, dtype=jnp.int32)
    a_meta = jnp.where(slots_a < a_count[:, :, None], a_index, -2)
    slots_c = jnp.arange(SC, dtype=jnp.int32)
    c_meta = half(jnp.where(slots_c < c_count[:, :, None], c_cols, -1), 0)[:, 0]
    b_own = b_blocks[0, 0]

    b_low = shift_y(b_own[: MB // 2], 1)
    b_high = shift_y(b_own[MB // 2 :], -1)
    other = shift_y(own, 1)
    a_all = lax.all_gather(half(a_blocks, 0).reshape(PAIR, BS, BS), COL)

    a_meta = half(lax.all_gather(a_meta, COL), 1).reshape(NZ, PAIR)
    a_meta = jnp.pad(a_meta, ((0, 0), (0, LANES - PAIR)), constant_values=-2)
    c_meta = jnp.broadcast_to(c_meta.T[:, :, None], (SC, ROWS, PAIR // ROWS)).reshape(SC, PAIR)
    c_meta = jnp.pad(c_meta, ((0, 0), (0, LANES - PAIR)), constant_values=-1).reshape(1, SC * LANES)
    meta = jnp.concatenate([a_meta, jnp.broadcast_to(c_meta, (NZ, SC * LANES))], axis=1)
    meta = spread(meta, "z")

    first = (0, CAP)
    msgs = spread(pack(meta, own, other, b_own, b_low, b_high, *first), "z")
    out, longest = consume(a_all, [msgs], [first])

    def again(_):
        rest = (CAP, PAIR - CAP)
        more = spread(pack(meta, own, other, b_own, b_low, b_high, *rest), "z")
        return consume(a_all, [msgs, more], [first, rest])[0]

    out = lax.cond(longest[0, 0] > CAP, again, lambda done: done, out)
    return out.reshape(ROWS, 1, SC, BS, BS)


def solution(mesh):
    fine = Mesh(mesh.devices.reshape(NZ, NYL, NX, NCORE, NREP), AXES)
    row = ("z", "yl")
    return jax.shard_map(
        body,
        mesh=fine,
        in_specs=tuple(
            P(row, COL, *([None] * (rank - 2))) for rank in (5, 3, 2, 5, 3, 3, 2, 3, 2)
        ),
        out_specs=P(("z", "yl", "rep"), COL, None, None, None),
        check_vma=False,
    )
```

```python
import functools

import jax
import jax.numpy as jnp
from jax import lax
from jax.experimental import pallas as pl
from jax.experimental.pallas import tpu as pltpu
from jax.sharding import Mesh
from jax.sharding import PartitionSpec as P

NZ, NYL, NX, NCORE, NREP = 8, 2, 4, 2, 2
AXES = ("z", "yl", "x", "core", "rep")
COL = ("x", "core")
BS, SA, SC, MB = 128, 2, 4, 32
ROWS = 4
PAIR = ROWS * 2 * SA
CAP = 10
HDR = 16
LANES = 128
SHIFTS = (0, 4, 3, -3, 2, -2, 1, -1)
EARLY = 4


def y_index(y):
    return (y % NYL) * NREP + y // NYL


def shift_y(value, steps):
    n = NYL * NREP
    return lax.ppermute(value, ("yl", "rep"), [(y_index(y), y_index((y + steps) % n)) for y in range(n)])


def shift_z(value, steps):
    if steps == 0:
        return value
    return lax.ppermute(value, "z", [(z, (z + steps) % NZ) for z in range(NZ)])


def pack_kernel(lo, size, meta, own, other, b_own, b_low, b_high, *rest):
    outs, (held, codes, scalars, sems) = rest[:NZ], rest[NZ:]
    copies = [
        pltpu.make_async_copy(b_own, held.at[pl.ds(0, MB)], sems.at[0]),
        pltpu.make_async_copy(b_low, held.at[pl.ds(MB, MB // 2)], sems.at[1]),
        pltpu.make_async_copy(b_high, held.at[pl.ds(MB + MB // 2, MB // 2)], sems.at[2]),
    ]
    for copy in copies:
        copy.start()
    yl = lax.axis_index("yl")
    me = lax.axis_index("z")
    col = lax.axis_index("x") * NCORE + lax.axis_index("core")
    lane = lax.broadcasted_iota(jnp.int32, (NZ, LANES), 1)
    is_own = ((lane >> 1) & 1) == yl
    first_half = lax.axis_index("rep") == 0
    wanted = jnp.concatenate([meta[z, pl.ds(me, 1), :] for z in range(NZ)], axis=0)
    wanted = jnp.where(first_half, wanted, pltpu.roll(wanted, LANES - PAIR, 1))
    wanted = jnp.where(lane < PAIR, wanted, -2)
    columns = jnp.concatenate([meta[z, pl.ds(col, 1), :] for z in range(NZ)], axis=0)
    columns = jnp.where(
        first_half,
        pltpu.roll(columns, LANES - 2 * PAIR, 1),
        pltpu.roll(columns, LANES - 2 * PAIR - ROWS * SC, 1),
    )
    moved = {d: pltpu.roll(columns, d % LANES, 1) for d in range(1 - SC, SC)}
    slot = jnp.zeros((NZ, LANES), jnp.int32)
    target = jnp.full((NZ, LANES), -5, jnp.int32)
    for m in range(MB):
        hit = wanted == jnp.where(is_own, own[0, m], other[0, m])
        slot = jnp.where(hit, m, slot)
        target = jnp.where(hit, jnp.where(is_own, own[1, m], other[1, m]), target)
    code = jnp.full((NZ, LANES), -1, jnp.int32)
    for s in range(SC):
        column = moved[-s]
        for o in range(1, SC):
            column = jnp.where((lane & (SC - 1)) == o, moved[o - s], column)
        code = jnp.where(column == target, slot * SC + s, code)
    codes[...] = code
    to_scalars = pltpu.make_async_copy(codes, scalars, sems.at[3])
    to_scalars.start()
    head = jnp.concatenate([code, jnp.full((HDR - NZ, LANES), -1, jnp.int32)], axis=0)
    head = head.astype(jnp.float32).astype(jnp.bfloat16)
    for out in outs:
        out[pl.ds(size * BS, HDR), :] = head
    to_scalars.wait()
    for copy in copies:
        copy.wait()
    for out, shift in zip(outs, SHIFTS):
        z = lax.rem(me + (NZ + shift), NZ)

        def step(t, count, out=out, z=z):
            code = scalars[z, t]
            hit = code >= 0

            @pl.when(hit & (count >= lo) & (count < lo + size))
            def _():
                block = (code >> 2) + jnp.where(((t >> 1) & 1) == yl, 0, MB)
                out[pl.ds(pl.multiple_of((count - lo) * BS, BS), BS), :] = held[block]

            return count + hit.astype(jnp.int32)

        lax.fori_loop(0, PAIR, step, jnp.int32(0))


def pack(meta, own, other, b_own, b_low, b_high, lo, size):
    smem, vmem, hbm = (pl.BlockSpec(memory_space=m) for m in (pltpu.SMEM, pltpu.VMEM, pl.ANY))
    return pl.pallas_call(
        functools.partial(pack_kernel, lo, size),
        out_shape=[jax.ShapeDtypeStruct((size * BS + HDR, BS), jnp.bfloat16)] * NZ,
        in_specs=[vmem, smem, smem, hbm, hbm, hbm],
        out_specs=[vmem] * NZ,
        scratch_shapes=[
            pltpu.VMEM((2 * MB, BS, BS), jnp.bfloat16),
            pltpu.VMEM((NZ, LANES), jnp.int32),
            pltpu.SMEM((NZ, LANES), jnp.int32),
            pltpu.SemaphoreType.DMA((4,)),
        ],
        compiler_params=pltpu.CompilerParams(vmem_limit_bytes=24 * 2**20),
        name="pack",
    )(meta, own, other, b_own, b_low, b_high)


def consume_kernel(shifts, parts, final, a_all, total_in, longest_in, *rest):
    count_msgs = len(shifts) * len(parts)
    msgs, (out, longest, total, codes, scalars, sem) = rest[:count_msgs], rest[count_msgs:]
    me = lax.axis_index("z")
    row = lax.broadcasted_iota(jnp.int32, (HDR, LANES), 0)
    most = jnp.zeros((HDR, 1), jnp.int32)
    for n in range(len(shifts)):
        head = msgs[n * len(parts)][pl.ds(parts[0][1] * BS, HDR), :].astype(jnp.float32).astype(jnp.int32)
        codes[pl.ds(n, 1), :] = jnp.sum(jnp.where(row == me, head, 0), axis=0, keepdims=True)
        most = jnp.maximum(most, jnp.sum((head >= 0).astype(jnp.int32), axis=1, keepdims=True))
    to_scalars = pltpu.make_async_copy(codes, scalars, sem)
    to_scalars.start()
    most = jnp.broadcast_to(jnp.max(most, axis=0, keepdims=True), longest.shape)
    longest[...] = jnp.maximum(most, longest_in[...])
    total[...] = total_in[...]
    to_scalars.wait()
    for n, shift in enumerate(shifts):
        source = lax.rem(me + (NZ - shift), NZ)

        def step(t, count, n=n, source=source):
            code = scalars[n, t]
            hit = code >= 0
            place = (t >> 2) * SC + (code & 3)
            for part, (lo, size) in enumerate(parts):

                @pl.when(hit & (count >= lo) & (count < lo + size))
                def _(lo=lo, msg=msgs[n * len(parts) + part]):
                    block = msg[pl.ds(pl.multiple_of((count - lo) * BS, BS), BS), :]
                    total[place] += jnp.dot(a_all[source, t], block, preferred_element_type=jnp.float32)

            return count + hit.astype(jnp.int32)

        lax.fori_loop(0, PAIR, step, jnp.int32(0))
    if final:
        out[...] = total[...].astype(out.dtype)
    else:
        out[...] = total[...]


def consume(a_all, total, longest, shifts, parts, msgs, final):
    vmem = pl.BlockSpec(memory_space=pltpu.VMEM)
    shape = (ROWS * SC, BS, BS)
    return pl.pallas_call(
        functools.partial(consume_kernel, shifts, parts, final),
        out_shape=(
            jax.ShapeDtypeStruct(shape, jnp.bfloat16 if final else jnp.float32),
            jax.ShapeDtypeStruct((8, LANES), jnp.int32),
        ),
        in_specs=[vmem] * (3 + len(msgs)),
        out_specs=(vmem, vmem),
        scratch_shapes=[
            pltpu.VMEM(shape, jnp.float32),
            pltpu.VMEM((NZ, LANES), jnp.int32),
            pltpu.SMEM((NZ, LANES), jnp.int32),
            pltpu.SemaphoreType.DMA,
        ],
        compiler_params=pltpu.CompilerParams(vmem_limit_bytes=24 * 2**20),
        cost_estimate=pl.CostEstimate(flops=2 * BS**3 * 40, bytes_accessed=8 * 2**20, transcendentals=0),
        name="consume",
    )(a_all, total, longest, *msgs)


def body(a_blocks, a_index, a_count, b_blocks, b_rows, b_cols, b_count, c_cols, c_count):
    rep = lax.axis_index("rep")

    slots_b = jnp.arange(MB, dtype=jnp.int32)
    own = jnp.stack([jnp.where(slots_b < b_count[0, 0], b_rows[0, 0], -1), b_cols[0, 0]])
    slots_a = jnp.arange(SA, dtype=jnp.int32)
    a_meta = jnp.where(slots_a < a_count[:, :, None], a_index, -2)
    slots_c = jnp.arange(SC, dtype=jnp.int32)
    c_meta = jnp.where(slots_c < c_count[:, :, None], c_cols, -1)
    b_own = b_blocks[0, 0]

    other = shift_y(own, 1)
    b_low = shift_y(b_own[: MB // 2], 1)
    b_high = shift_y(b_own[MB // 2 :], -1)

    meta = jnp.concatenate([a_meta.reshape(2 * PAIR), c_meta.reshape(2 * ROWS * SC)])
    meta = jnp.pad(meta, (0, LANES - meta.shape[0]))
    meta = jnp.broadcast_to(meta[None, :], (NZ * NX * NCORE, LANES))
    meta = lax.all_to_all(meta, ("z", "x", "core"), 0, 0).reshape(NZ, NX * NCORE, LANES)

    start = rep * ROWS + jnp.minimum(meta[0, 0, 0] + 2, 0)
    a_all = lax.dynamic_slice_in_dim(a_blocks, start, ROWS, 0).reshape(PAIR, BS, BS)
    a_all = lax.all_gather(a_all, COL)

    def send(lo, size):
        outs = pack(meta, own, other, b_own, b_low, b_high, lo, size)
        return [shift_z(out, shift) for out, shift in zip(outs, SHIFTS)]

    first = (0, CAP)
    msgs = send(*first)
    total = jnp.zeros((ROWS * SC, BS, BS), jnp.float32)
    longest = jnp.zeros((8, LANES), jnp.int32)
    total, longest = consume(a_all, total, longest, SHIFTS[:EARLY], [first], msgs[:EARLY], False)
    out, longest = consume(a_all, total, longest, SHIFTS[EARLY:], [first], msgs[EARLY:], True)

    def again(_):
        rest = (CAP, PAIR - CAP)
        both = [msg for pair in zip(msgs, send(*rest)) for msg in pair]
        zero = jnp.zeros((ROWS * SC, BS, BS), jnp.float32)
        return consume(a_all, zero, longest, SHIFTS, [first, rest], both, True)[0]

    out = lax.cond(longest[0, 0] > CAP, again, lambda done: done, out)
    return out.reshape(ROWS, 1, SC, BS, BS)


def solution(mesh):
    fine = Mesh(mesh.devices.reshape(NZ, NYL, NX, NCORE, NREP), AXES)
    row = ("z", "yl")
    return jax.shard_map(
        body,
        mesh=fine,
        in_specs=tuple(
            P(row, COL, *([None] * (rank - 2))) for rank in (5, 3, 2, 5, 3, 3, 2, 3, 2)
        ),
        out_specs=P(("z", "yl", "rep"), COL, None, None, None),
        check_vma=False,
    )
```

```python
import functools

import jax
import jax.numpy as jnp
from jax import lax
from jax.experimental import pallas as pl
from jax.experimental.pallas import tpu as pltpu
from jax.sharding import Mesh
from jax.sharding import PartitionSpec as P

NZ, NYL, NX, NCORE, NREP = 8, 2, 4, 2, 2
AXES = ("z", "yl", "x", "core", "rep")
COL = ("x", "core")
BS, SA, SC, MB = 128, 2, 4, 32
ROWS = 4
PAIR = ROWS * 2 * SA
CAP = 10
HDR = 16
LANES = 128
SHIFTS = (0, 4, 3, -3, 2, -2, 1, -1)
EARLY = 4


def y_index(y):
    return (y % NYL) * NREP + y // NYL


def shift_y(value, steps):
    n = NYL * NREP
    return lax.ppermute(value, ("yl", "rep"), [(y_index(y), y_index((y + steps) % n)) for y in range(n)])


def shift_z(value, steps):
    if steps == 0:
        return value
    return lax.ppermute(value, "z", [(z, (z + steps) % NZ) for z in range(NZ)])


def pack_kernel(lo, size, meta, own, other, b_own, b_low, b_high, *rest):
    outs, (held, codes, scalars, sems) = rest[:NZ], rest[NZ:]
    copies = [
        pltpu.make_async_copy(b_own, held.at[pl.ds(0, MB)], sems.at[0]),
        pltpu.make_async_copy(b_low, held.at[pl.ds(MB, MB // 2)], sems.at[1]),
        pltpu.make_async_copy(b_high, held.at[pl.ds(MB + MB // 2, MB // 2)], sems.at[2]),
    ]
    for copy in copies:
        copy.start()
    yl = lax.axis_index("yl")
    me = lax.axis_index("z")
    col = lax.axis_index("x") * NCORE + lax.axis_index("core")
    lane = lax.broadcasted_iota(jnp.int32, (NZ, LANES), 1)
    is_own = ((lane >> 1) & 1) == yl
    first_half = lax.axis_index("rep") == 0
    wanted = jnp.concatenate([meta[z, pl.ds(me, 1), :] for z in range(NZ)], axis=0)
    wanted = jnp.where(first_half, wanted, pltpu.roll(wanted, LANES - PAIR, 1))
    wanted = jnp.where(lane < PAIR, wanted, -2)
    columns = jnp.concatenate([meta[z, pl.ds(col, 1), :] for z in range(NZ)], axis=0)
    columns = jnp.where(
        first_half,
        pltpu.roll(columns, LANES - 2 * PAIR, 1),
        pltpu.roll(columns, LANES - 2 * PAIR - ROWS * SC, 1),
    )
    moved = {d: pltpu.roll(columns, d % LANES, 1) for d in range(1 - SC, SC)}
    slot = jnp.zeros((NZ, LANES), jnp.int32)
    target = jnp.full((NZ, LANES), -5, jnp.int32)
    for m in range(MB):
        hit = wanted == jnp.where(is_own, own[0, m], other[0, m])
        slot = jnp.where(hit, m, slot)
        target = jnp.where(hit, jnp.where(is_own, own[1, m], other[1, m]), target)
    code = jnp.full((NZ, LANES), -1, jnp.int32)
    for s in range(SC):
        column = moved[-s]
        for o in range(1, SC):
            column = jnp.where((lane & (SC - 1)) == o, moved[o - s], column)
        code = jnp.where(column == target, slot * SC + s, code)
    codes[...] = code
    to_scalars = pltpu.make_async_copy(codes, scalars, sems.at[3])
    to_scalars.start()
    head = jnp.concatenate([code, jnp.full((HDR - NZ, LANES), -1, jnp.int32)], axis=0)
    head = head.astype(jnp.float32).astype(jnp.bfloat16)
    for out in outs:
        out[pl.ds(size * BS, HDR), :] = head
    to_scalars.wait()
    for copy in copies:
        copy.wait()
    for out, shift in zip(outs, SHIFTS):
        z = lax.rem(me + (NZ + shift), NZ)

        def step(t, count, out=out, z=z):
            code = scalars[z, t]
            hit = code >= 0

            @pl.when(hit & (count >= lo) & (count < lo + size))
            def _():
                block = (code >> 2) + jnp.where(((t >> 1) & 1) == yl, 0, MB)
                out[pl.ds(pl.multiple_of((count - lo) * BS, BS), BS), :] = held[block]

            return count + hit.astype(jnp.int32)

        lax.fori_loop(0, PAIR, step, jnp.int32(0))


def pack(meta, own, other, b_own, b_low, b_high, lo, size):
    smem, vmem, hbm = (pl.BlockSpec(memory_space=m) for m in (pltpu.SMEM, pltpu.VMEM, pl.ANY))
    return pl.pallas_call(
        functools.partial(pack_kernel, lo, size),
        out_shape=[jax.ShapeDtypeStruct((size * BS + HDR, BS), jnp.bfloat16)] * NZ,
        in_specs=[vmem, smem, smem, hbm, hbm, hbm],
        out_specs=[vmem] * NZ,
        scratch_shapes=[
            pltpu.VMEM((2 * MB, BS, BS), jnp.bfloat16),
            pltpu.VMEM((NZ, LANES), jnp.int32),
            pltpu.SMEM((NZ, LANES), jnp.int32),
            pltpu.SemaphoreType.DMA((4,)),
        ],
        compiler_params=pltpu.CompilerParams(vmem_limit_bytes=24 * 2**20),
        name="pack",
    )(meta, own, other, b_own, b_low, b_high)


def consume_kernel(shifts, parts, final, a_all, total_in, longest_in, *rest):
    count_msgs = len(shifts) * len(parts)
    msgs, (out, longest, total, codes, scalars, sem) = rest[:count_msgs], rest[count_msgs:]
    me = lax.axis_index("z")
    row = lax.broadcasted_iota(jnp.int32, (HDR, LANES), 0)
    most = jnp.zeros((HDR, 1), jnp.int32)
    for n in range(len(shifts)):
        head = msgs[n * len(parts)][pl.ds(parts[0][1] * BS, HDR), :].astype(jnp.float32).astype(jnp.int32)
        codes[pl.ds(n, 1), :] = jnp.sum(jnp.where(row == me, head, 0), axis=0, keepdims=True)
        most = jnp.maximum(most, jnp.sum((head >= 0).astype(jnp.int32), axis=1, keepdims=True))
    to_scalars = pltpu.make_async_copy(codes, scalars, sem)
    to_scalars.start()
    most = jnp.broadcast_to(jnp.max(most, axis=0, keepdims=True), longest.shape)
    longest[...] = jnp.maximum(most, longest_in[...])
    total[...] = total_in[...]
    to_scalars.wait()
    for n, shift in enumerate(shifts):
        source = lax.rem(me + (NZ - shift), NZ)

        def step(t, count, n=n, source=source):
            code = scalars[n, t]
            hit = code >= 0
            place = (t >> 2) * SC + (code & 3)
            for part, (lo, size) in enumerate(parts):

                @pl.when(hit & (count >= lo) & (count < lo + size))
                def _(lo=lo, msg=msgs[n * len(parts) + part]):
                    block = msg[pl.ds(pl.multiple_of((count - lo) * BS, BS), BS), :]
                    total[place] += jnp.dot(a_all[source, t], block, preferred_element_type=jnp.float32)

            return count + hit.astype(jnp.int32)

        lax.fori_loop(0, PAIR, step, jnp.int32(0))
    if final:
        out[...] = total[...].astype(out.dtype)
    else:
        out[...] = total[...]


def consume(a_all, total, longest, shifts, parts, msgs, final):
    vmem = pl.BlockSpec(memory_space=pltpu.VMEM)
    shape = (ROWS * SC, BS, BS)
    return pl.pallas_call(
        functools.partial(consume_kernel, shifts, parts, final),
        out_shape=(
            jax.ShapeDtypeStruct(shape, jnp.bfloat16 if final else jnp.float32),
            jax.ShapeDtypeStruct((8, LANES), jnp.int32),
        ),
        in_specs=[vmem] * (3 + len(msgs)),
        out_specs=(vmem, vmem),
        scratch_shapes=[
            pltpu.VMEM(shape, jnp.float32),
            pltpu.VMEM((NZ, LANES), jnp.int32),
            pltpu.SMEM((NZ, LANES), jnp.int32),
            pltpu.SemaphoreType.DMA,
        ],
        compiler_params=pltpu.CompilerParams(vmem_limit_bytes=24 * 2**20),
        cost_estimate=pl.CostEstimate(flops=2 * BS**3 * 40, bytes_accessed=8 * 2**20, transcendentals=0),
        name="consume",
    )(a_all, total, longest, *msgs)


def body(a_blocks, a_index, a_count, b_blocks, b_rows, b_cols, b_count, c_cols, c_count):
    rep = lax.axis_index("rep")

    slots_b = jnp.arange(MB, dtype=jnp.int32)
    own = jnp.stack([jnp.where(slots_b < b_count[0, 0], b_rows[0, 0], -1), b_cols[0, 0]])
    slots_a = jnp.arange(SA, dtype=jnp.int32)
    a_meta = jnp.where(slots_a < a_count[:, :, None], a_index, -2)
    slots_c = jnp.arange(SC, dtype=jnp.int32)
    c_meta = jnp.where(slots_c < c_count[:, :, None], c_cols, -1)
    b_own = b_blocks[0, 0]

    a_all = lax.dynamic_slice_in_dim(a_blocks, rep * ROWS, ROWS, 0).reshape(PAIR, BS, BS)
    a_all = lax.all_gather(a_all, COL)

    other = shift_y(own, 1)
    b_low = shift_y(b_own[: MB // 2], 1)
    b_high = shift_y(b_own[MB // 2 :], -1)

    meta = jnp.concatenate([a_meta.reshape(2 * PAIR), c_meta.reshape(2 * ROWS * SC)])
    meta = jnp.pad(meta, (0, LANES - meta.shape[0]))
    meta = jnp.broadcast_to(meta[None, :], (NZ * NX * NCORE, LANES))
    meta = lax.all_to_all(meta, ("z", "x", "core"), 0, 0).reshape(NZ, NX * NCORE, LANES)

    def send(lo, size):
        outs = pack(meta, own, other, b_own, b_low, b_high, lo, size)
        return [shift_z(out, shift) for out, shift in zip(outs, SHIFTS)]

    first = (0, CAP)
    msgs = send(*first)
    total = jnp.zeros((ROWS * SC, BS, BS), jnp.float32)
    longest = jnp.zeros((8, LANES), jnp.int32)
    total, longest = consume(a_all, total, longest, SHIFTS[:EARLY], [first], msgs[:EARLY], False)
    out, longest = consume(a_all, total, longest, SHIFTS[EARLY:], [first], msgs[EARLY:], True)

    def again(_):
        rest = (CAP, PAIR - CAP)
        both = [msg for pair in zip(msgs, send(*rest)) for msg in pair]
        zero = jnp.zeros((ROWS * SC, BS, BS), jnp.float32)
        return consume(a_all, zero, longest, SHIFTS, [first, rest], both, True)[0]

    out = lax.cond(longest[0, 0] > CAP, again, lambda done: done, out)
    return out.reshape(ROWS, 1, SC, BS, BS)


def solution(mesh):
    fine = Mesh(mesh.devices.reshape(NZ, NYL, NX, NCORE, NREP), AXES)
    row = ("z", "yl")
    return jax.shard_map(
        body,
        mesh=fine,
        in_specs=tuple(
            P(row, COL, *([None] * (rank - 2))) for rank in (5, 3, 2, 5, 3, 3, 2, 3, 2)
        ),
        out_specs=P(("z", "yl", "rep"), COL, None, None, None),
        check_vma=False,
    )
```

```python
import functools

import jax
import jax.numpy as jnp
from jax import lax
from jax.experimental import pallas as pl
from jax.experimental.pallas import tpu as pltpu
from jax.sharding import Mesh
from jax.sharding import PartitionSpec as P

NZ, NYL, NX, NCORE, NREP = 8, 2, 4, 2, 2
AXES = ("z", "yl", "x", "core", "rep")
COL = ("x", "core")
BS, SA, SC, MB = 128, 2, 4, 32
ROWS = 4
PAIR = ROWS * 2 * SA
CAP = 8
HDR = 16
LANES = 128
SHIFTS = (0, 4, 3, -3, 2, -2, 1, -1)
EARLY = 4


def along_y(value, steps, other_core):
    n = NYL * NREP
    pairs = []
    for y in range(n):
        for core in range(NCORE):
            ends = []
            for where, at in ((y, core), ((y + steps) % n, core ^ other_core)):
                ends.append(((where % NYL) * NCORE + at) * NREP + where // NYL)
            pairs.append(tuple(ends))
    return lax.ppermute(value, ("yl", "core", "rep"), pairs)


def shift_z(value, steps):
    if steps == 0:
        return value
    return lax.ppermute(value, "z", [(z, (z + steps) % NZ) for z in range(NZ)])


def swap(value):
    return lax.ppermute(value, "core", [(0, 1), (1, 0)])


def find_codes(wanted, columns, own, other, is_own, lane):
    slot = jnp.zeros((NZ, LANES), jnp.int32)
    target = jnp.full((NZ, LANES), -5, jnp.int32)
    for m in range(MB):
        hit = wanted == jnp.where(is_own, own[0, m], other[0, m])
        slot = jnp.where(hit, m, slot)
        target = jnp.where(hit, jnp.where(is_own, own[1, m], other[1, m]), target)
    moved = {d: pltpu.roll(columns, d % LANES, 1) if d else columns for d in range(1 - SC, SC)}
    code = jnp.full((NZ, LANES), -1, jnp.int32)
    for s in range(SC):
        column = moved[-s]
        for o in range(1, SC):
            column = jnp.where((lane & (SC - 1)) == o, moved[o - s], column)
        code = jnp.where(column == target, slot * SC + s, code)
    return code


def pack_kernel(shifts, lo, size, meta, own, other, twin_other, *rest):
    lists, outs = rest[:4], rest[4 : 4 + len(shifts)]
    held, codes, scalars, sems = rest[4 + len(shifts) :]
    core = lax.axis_index("core")
    mine, twins = core * 2 * MB, (1 - core) * 2 * MB
    copies = []
    for n, (source, first) in enumerate(zip(lists, (mine, mine + MB, twins, twins + MB))):
        copies.append(pltpu.make_async_copy(source, held.at[pl.ds(first, MB)], sems.at[n]))
        copies[-1].start()
    yl = lax.axis_index("yl")
    me = lax.axis_index("z")
    x = lax.axis_index("x")
    lane = lax.broadcasted_iota(jnp.int32, (NZ, LANES), 1)
    is_own = ((lane >> 1) & 1) == yl
    first_half = lax.axis_index("rep") == 0

    def pick(col, start, length):
        rows = jnp.concatenate([meta[z, pl.ds(col, 1), :] for z in range(NZ)], axis=0)
        low = pltpu.roll(rows, LANES - start, 1) if start else rows
        return jnp.where(first_half, low, pltpu.roll(rows, LANES - start - length, 1))

    wanted = jnp.where(lane < PAIR, pick(me, 0, PAIR), -2)
    twin_meta = meta[me, pl.ds(x * NCORE + 1 - core, 1), :]
    twin_own = {
        (n, m): twin_meta[:, 4 * PAIR + n * MB + m : 4 * PAIR + n * MB + m + 1] for n in range(2) for m in range(MB)
    }
    code = find_codes(wanted, pick(x * NCORE + core, 2 * PAIR, ROWS * SC), own, other, is_own, lane)
    twin = find_codes(wanted, pick(x * NCORE + 1 - core, 2 * PAIR, ROWS * SC), twin_own, twin_other, is_own, lane)
    code, twin = jnp.where(core == 0, code, twin), jnp.where(core == 0, twin, code)
    code = jnp.where(lane < PAIR, code, jnp.where(lane < 2 * PAIR, pltpu.roll(twin, PAIR, 1), -1))
    codes[...] = code
    to_scalars = pltpu.make_async_copy(codes, scalars, sems.at[4])
    to_scalars.start()
    head = jnp.concatenate([code, jnp.full((HDR - NZ, LANES), -1, jnp.int32)], axis=0)
    head = head.astype(jnp.float32).astype(jnp.bfloat16)
    for out, shift in zip(outs, shifts):
        out[pl.ds((size if shift else PAIR) * BS, HDR), :] = head
    to_scalars.wait()
    for copy in copies:
        copy.wait()

    def block(t, code):
        return (t >> 4) * (2 * MB) + jnp.where(((t >> 1) & 1) == yl, 0, MB) + (code >> 2)

    for out, shift in zip(outs, shifts):
        z = lax.rem(me + (NZ + shift), NZ)

        def step(t, count, out=out, z=z):
            code = scalars[z, t]
            hit = code >= 0
            place = count >> 1

            @pl.when(hit & ((count & 1) == core) & (place >= lo) & (place < lo + size))
            def _():
                out[pl.ds(pl.multiple_of((place - lo) * BS, BS), BS), :] = held[block(t, code)]

            return count + hit.astype(jnp.int32)

        def steps(n, count, step=step):
            for k in range(8):
                count = step(n * 8 + k, count)
            return count

        def own_step(t, count, out=out, z=z):
            t = core * PAIR + t
            code = scalars[z, t]
            hit = code >= 0

            @pl.when(hit)
            def _():
                out[pl.ds(pl.multiple_of(count * BS, BS), BS), :] = held[block(t, code)]

            return count + hit.astype(jnp.int32)

        if shift:
            lax.fori_loop(0, 2 * PAIR // 8, steps, jnp.int32(0))
        else:
            lax.fori_loop(0, PAIR, own_step, jnp.int32(0))


def pack(meta, lists, blocks, shifts, lo, size):
    smem, vmem, hbm = (pl.BlockSpec(memory_space=m) for m in (pltpu.SMEM, pltpu.VMEM, pl.ANY))
    return pl.pallas_call(
        functools.partial(pack_kernel, shifts, lo, size),
        out_shape=[
            jax.ShapeDtypeStruct(((size if shift else PAIR) * BS + HDR, BS), jnp.bfloat16)
            for shift in shifts
        ],
        in_specs=[vmem] + [smem] * 3 + [hbm] * 4,
        out_specs=[vmem] * len(shifts),
        scratch_shapes=[
            pltpu.VMEM((4 * MB, BS, BS), jnp.bfloat16),
            pltpu.VMEM((NZ, LANES), jnp.int32),
            pltpu.SMEM((NZ, LANES), jnp.int32),
            pltpu.SemaphoreType.DMA((5,)),
        ],
        compiler_params=pltpu.CompilerParams(vmem_limit_bytes=28 * 2**20),
        name="pack",
    )(meta, *lists, *blocks)


def consume_kernel(shifts, parts, a_all, own_in, twin_in, longest_in, *rest):
    width = {shift: len(parts) if shift else 1 for shift in shifts}
    count_msgs = sum(width.values())
    msgs, (own_out, twin_out, longest, totals, codes, scalars, sem) = rest[:count_msgs], rest[count_msgs:]
    n_sums = ROWS * SC
    groups = {}
    for shift in shifts:
        groups[shift], msgs = msgs[: width[shift]], msgs[width[shift] :]
    me = lax.axis_index("z")
    core = lax.axis_index("core")
    row = lax.broadcasted_iota(jnp.int32, (HDR, LANES), 0)
    most = jnp.zeros((HDR, 1), jnp.int32)
    for n, shift in enumerate(shifts):
        source = lax.rem(me + (NZ - shift), NZ)
        head = groups[shift][0][pl.ds((parts[0][1] if shift else PAIR) * BS, HDR), :]
        head = head.astype(jnp.float32).astype(jnp.int32)
        codes[pl.ds(n, 1), :] = jnp.sum(jnp.where(row == me, head, 0), axis=0, keepdims=True)
        sent = (head >= 0) & (row != source)
        most = jnp.maximum(most, jnp.sum(sent.astype(jnp.int32), axis=1, keepdims=True))
    to_scalars = pltpu.make_async_copy(codes, scalars, sem)
    to_scalars.start()
    most = jnp.broadcast_to(jnp.max(most, axis=0, keepdims=True), longest.shape)
    longest[...] = jnp.maximum(most, longest_in[...])
    totals[:n_sums] = own_in[...]
    totals[n_sums:] = twin_in[...]
    to_scalars.wait()

    def add(wanted, whose, source, t, code, msg, place):
        @pl.when(wanted)
        def _():
            block = msg[pl.ds(pl.multiple_of(place * BS, BS), BS), :]
            target = whose * n_sums + (t >> 2) * SC + (code & 3)
            totals[target] += jnp.dot(a_all[source, t], block, preferred_element_type=jnp.float32)

    for n, shift in enumerate(shifts):
        source = lax.rem(me + (NZ - shift), NZ)
        group = groups[shift]

        def step(t, count, n=n, source=source, group=group):
            code = scalars[n, t]
            hit = code >= 0
            place = count >> 1
            whose = (t >> 4) ^ core
            for (lo, size), msg in zip(parts, group):
                here = hit & ((count & 1) == core) & (place >= lo) & (place < lo + size)
                add(here, whose, source, t & (PAIR - 1), code, msg, place - lo)
            return count + hit.astype(jnp.int32)

        def own_step(t, count, n=n, source=source, group=group):
            code = scalars[n, core * PAIR + t]
            hit = code >= 0
            add(hit, 0, source, t, code, group[0], count)
            return count + hit.astype(jnp.int32)

        if shift:
            lax.fori_loop(0, 2 * PAIR, step, jnp.int32(0))
        else:
            lax.fori_loop(0, PAIR, own_step, jnp.int32(0))
    own_out[...] = totals[:n_sums]
    twin_out[...] = totals[n_sums:]


def consume(a_all, sums, longest, shifts, parts, msgs):
    vmem = pl.BlockSpec(memory_space=pltpu.VMEM)
    return pl.pallas_call(
        functools.partial(consume_kernel, shifts, parts),
        out_shape=(
            jax.ShapeDtypeStruct((ROWS * SC, BS, BS), jnp.float32),
            jax.ShapeDtypeStruct((ROWS * SC, BS, BS), jnp.float32),
            jax.ShapeDtypeStruct((8, LANES), jnp.int32),
        ),
        in_specs=[vmem] * (4 + len(msgs)),
        out_specs=(vmem, vmem, vmem),
        scratch_shapes=[
            pltpu.VMEM((2 * ROWS * SC, BS, BS), jnp.float32),
            pltpu.VMEM((NZ, LANES), jnp.int32),
            pltpu.SMEM((NZ, LANES), jnp.int32),
            pltpu.SemaphoreType.DMA,
        ],
        compiler_params=pltpu.CompilerParams(vmem_limit_bytes=28 * 2**20),
        cost_estimate=pl.CostEstimate(flops=2 * BS**3 * 40, bytes_accessed=8 * 2**20, transcendentals=0),
        name="consume",
    )(a_all, *sums, longest, *msgs)


def body(a_blocks, a_index, a_count, b_blocks, b_rows, b_cols, b_count, c_cols, c_count):
    rep = lax.axis_index("rep")
    a_all = lax.dynamic_slice_in_dim(a_blocks, rep * ROWS, ROWS, 0).reshape(PAIR, BS, BS)
    a_all = lax.all_gather(a_all, COL)

    slots_b = jnp.arange(MB, dtype=jnp.int32)
    own = jnp.stack([jnp.where(slots_b < b_count[0, 0], b_rows[0, 0], -1), b_cols[0, 0]])
    slots_a = jnp.arange(SA, dtype=jnp.int32)
    a_meta = jnp.where(slots_a < a_count[:, :, None], a_index, -2)
    slots_c = jnp.arange(SC, dtype=jnp.int32)
    c_meta = jnp.where(slots_c < c_count[:, :, None], c_cols, -1)
    b_own = b_blocks[0, 0]

    blocks = [b_own, along_y(b_own, 1, 0), swap(b_own), along_y(b_own, -1, 1)]
    lists = [own, along_y(own, 1, 0), along_y(own, -1, 1)]

    meta = jnp.concatenate([a_meta.reshape(2 * PAIR), c_meta.reshape(2 * ROWS * SC), own.reshape(2 * MB)])
    meta = jnp.broadcast_to(meta[None, :], (NZ * NX * NCORE, LANES))
    meta = lax.all_to_all(meta, ("z", "x", "core"), 0, 0).reshape(NZ, NX * NCORE, LANES)

    def send(shifts, lo, size):
        outs = pack(meta, lists, blocks, shifts, lo, size)
        return [shift_z(out, shift) for out, shift in zip(outs, shifts)]

    def finish(own_sums, twin_sums):
        return (own_sums + twin_sums).astype(jnp.bfloat16)

    first = (0, CAP)
    msgs = send(SHIFTS, *first)
    zero = [jnp.zeros((ROWS * SC, BS, BS), jnp.float32)] * 2
    longest = jnp.zeros((8, LANES), jnp.int32)
    *sums, longest = consume(a_all, zero, longest, SHIFTS[:EARLY], [first], msgs[:EARLY])
    *sums, longest = consume(a_all, sums, longest, SHIFTS[EARLY:], [first], msgs[EARLY:])

    def again(*_):
        rest = (CAP, PAIR - CAP)
        both = msgs[:1] + [m for pair in zip(msgs[1:], send(SHIFTS[1:], *rest)) for m in pair]
        own_sums, twin_sums, _ = consume(a_all, zero, longest, SHIFTS, [first, rest], both)
        return finish(own_sums, swap(twin_sums))

    out = lax.cond(longest[0, 0] > 2 * CAP, again, finish, sums[0], swap(sums[1]))
    return out.reshape(ROWS, 1, SC, BS, BS)


def solution(mesh):
    fine = Mesh(mesh.devices.reshape(NZ, NYL, NX, NCORE, NREP), AXES)
    row = ("z", "yl")
    return jax.shard_map(
        body,
        mesh=fine,
        in_specs=tuple(
            P(row, COL, *([None] * (rank - 2))) for rank in (5, 3, 2, 5, 3, 3, 2, 3, 2)
        ),
        out_specs=P(("z", "yl", "rep"), COL, None, None, None),
        check_vma=False,
    )
```

```python
import functools

import jax
import jax.numpy as jnp
from jax import lax
from jax.experimental import pallas as pl
from jax.experimental.pallas import tpu as pltpu
from jax.sharding import Mesh
from jax.sharding import PartitionSpec as P

NZ, NYL, NX, NCORE, NREP = 8, 2, 4, 2, 2
AXES = ("z", "yl", "x", "core", "rep")
COL = ("x", "core")
BS, SA, SC, MB = 128, 2, 4, 32
ROWS = 4
PAIR = ROWS * 2 * SA
CAP = 8
HDR = 16
LANES = 128
SHIFTS = (0, 4, 3, -3, 2, -2, 1, -1)
FAR = 5
EARLY = 4


def along_y(value, steps, other_core):
    n = NYL * NREP
    pairs = []
    for y in range(n):
        for core in range(NCORE):
            ends = []
            for where, at in ((y, core), ((y + steps) % n, core ^ other_core)):
                ends.append(((where % NYL) * NCORE + at) * NREP + where // NYL)
            pairs.append(tuple(ends))
    return lax.ppermute(value, ("yl", "core", "rep"), pairs)


def shift_z(value, steps):
    if steps == 0:
        return value
    return lax.ppermute(value, "z", [(z, (z + steps) % NZ) for z in range(NZ)])


def swap(value):
    return lax.ppermute(value, "core", [(0, 1), (1, 0)])


def find_codes(wanted, columns, own, other, is_own, lane):
    slot = jnp.zeros((NZ, LANES), jnp.int32)
    target = jnp.full((NZ, LANES), -5, jnp.int32)
    for m in range(MB):
        hit = wanted == jnp.where(is_own, own[0, m], other[0, m])
        slot = jnp.where(hit, m, slot)
        target = jnp.where(hit, jnp.where(is_own, own[1, m], other[1, m]), target)
    moved = {d: pltpu.roll(columns, d % LANES, 1) if d else columns for d in range(1 - SC, SC)}
    code = jnp.full((NZ, LANES), -1, jnp.int32)
    for s in range(SC):
        column = moved[-s]
        for o in range(1, SC):
            column = jnp.where((lane & (SC - 1)) == o, moved[o - s], column)
        code = jnp.where(column == target, slot * SC + s, code)
    return code


def pack_kernel(shifts, lo, size, meta, own, other, twin_other, *rest):
    lists, outs = rest[:4], rest[4 : 4 + len(shifts)]
    held, codes, scalars, sems = rest[4 + len(shifts) :]
    core = lax.axis_index("core")
    mine, twins = core * 2 * MB, (1 - core) * 2 * MB
    copies = []
    for n, (source, first) in enumerate(zip(lists, (mine, mine + MB, twins, twins + MB))):
        copies.append(pltpu.make_async_copy(source, held.at[pl.ds(first, MB)], sems.at[n]))
        copies[-1].start()
    yl = lax.axis_index("yl")
    me = lax.axis_index("z")
    x = lax.axis_index("x")
    lane = lax.broadcasted_iota(jnp.int32, (NZ, LANES), 1)
    is_own = ((lane >> 1) & 1) == yl
    first_half = lax.axis_index("rep") == 0

    def pick(col, start, length):
        rows = jnp.concatenate([meta[z, pl.ds(col, 1), :] for z in range(NZ)], axis=0)
        low = pltpu.roll(rows, LANES - start, 1) if start else rows
        return jnp.where(first_half, low, pltpu.roll(rows, LANES - start - length, 1))

    wanted = jnp.where(lane < PAIR, pick(me, 0, PAIR), -2)
    twin_meta = meta[me, pl.ds(x * NCORE + 1 - core, 1), :]
    twin_own = {
        (n, m): twin_meta[:, 4 * PAIR + n * MB + m : 4 * PAIR + n * MB + m + 1] for n in range(2) for m in range(MB)
    }
    code = find_codes(wanted, pick(x * NCORE + core, 2 * PAIR, ROWS * SC), own, other, is_own, lane)
    twin = find_codes(wanted, pick(x * NCORE + 1 - core, 2 * PAIR, ROWS * SC), twin_own, twin_other, is_own, lane)
    code, twin = jnp.where(core == 0, code, twin), jnp.where(core == 0, twin, code)
    code = jnp.where(lane < PAIR, code, jnp.where(lane < 2 * PAIR, pltpu.roll(twin, PAIR, 1), -1))
    codes[...] = code
    to_scalars = pltpu.make_async_copy(codes, scalars, sems.at[4])
    to_scalars.start()
    head = jnp.concatenate([code, jnp.full((HDR - NZ, LANES), -1, jnp.int32)], axis=0)
    head = head.astype(jnp.float32).astype(jnp.bfloat16)
    for out, shift in zip(outs, shifts):
        out[pl.ds((size if shift else PAIR) * BS, HDR), :] = head
    to_scalars.wait()
    for copy in copies:
        copy.wait()

    def block(t, code):
        return (t >> 4) * (2 * MB) + jnp.where(((t >> 1) & 1) == yl, 0, MB) + (code >> 2)

    for out, shift in zip(outs, shifts):
        z = lax.rem(me + (NZ + shift), NZ)

        def step(t, count, out=out, z=z):
            code = scalars[z, t]
            hit = code >= 0
            place = count >> 1

            @pl.when(hit & ((count & 1) == core) & (place >= lo) & (place < lo + size))
            def _():
                out[pl.ds(pl.multiple_of((place - lo) * BS, BS), BS), :] = held[block(t, code)]

            return count + hit.astype(jnp.int32)

        def steps(n, count, step=step):
            for k in range(8):
                count = step(n * 8 + k, count)
            return count

        def own_step(t, count, out=out, z=z):
            t = core * PAIR + t
            code = scalars[z, t]
            hit = code >= 0

            @pl.when(hit)
            def _():
                out[pl.ds(pl.multiple_of(count * BS, BS), BS), :] = held[block(t, code)]

            return count + hit.astype(jnp.int32)

        if shift:
            lax.fori_loop(0, 2 * PAIR // 8, steps, jnp.int32(0))
        else:
            lax.fori_loop(0, PAIR, own_step, jnp.int32(0))


def pack(meta, lists, blocks, shifts, lo, size):
    smem, vmem, hbm = (pl.BlockSpec(memory_space=m) for m in (pltpu.SMEM, pltpu.VMEM, pl.ANY))
    return pl.pallas_call(
        functools.partial(pack_kernel, shifts, lo, size),
        out_shape=[
            jax.ShapeDtypeStruct(((size if shift else PAIR) * BS + HDR, BS), jnp.bfloat16)
            for shift in shifts
        ],
        in_specs=[vmem] + [smem] * 3 + [hbm] * 4,
        out_specs=[vmem] * len(shifts),
        scratch_shapes=[
            pltpu.VMEM((4 * MB, BS, BS), jnp.bfloat16),
            pltpu.VMEM((NZ, LANES), jnp.int32),
            pltpu.SMEM((NZ, LANES), jnp.int32),
            pltpu.SemaphoreType.DMA((5,)),
        ],
        compiler_params=pltpu.CompilerParams(vmem_limit_bytes=28 * 2**20),
        name="pack",
    )(meta, *lists, *blocks)


def consume_kernel(shifts, parts, a_all, own_in, twin_in, longest_in, *rest):
    width = {shift: len(parts) if shift else 1 for shift in shifts}
    count_msgs = sum(width.values())
    msgs, (own_out, twin_out, longest, totals, codes, scalars, sem) = rest[:count_msgs], rest[count_msgs:]
    n_sums = ROWS * SC
    groups = {}
    for shift in shifts:
        groups[shift], msgs = msgs[: width[shift]], msgs[width[shift] :]
    me = lax.axis_index("z")
    core = lax.axis_index("core")
    row = lax.broadcasted_iota(jnp.int32, (HDR, LANES), 0)
    most = jnp.zeros((HDR, 1), jnp.int32)
    for n, shift in enumerate(shifts):
        source = lax.rem(me + (NZ - shift), NZ)
        head = groups[shift][0][pl.ds((parts[0][1] if shift else PAIR) * BS, HDR), :]
        head = head.astype(jnp.float32).astype(jnp.int32)
        codes[pl.ds(n, 1), :] = jnp.sum(jnp.where(row == me, head, 0), axis=0, keepdims=True)
        sent = (head >= 0) & (row != source)
        most = jnp.maximum(most, jnp.sum(sent.astype(jnp.int32), axis=1, keepdims=True))
    to_scalars = pltpu.make_async_copy(codes, scalars, sem)
    to_scalars.start()
    most = jnp.broadcast_to(jnp.max(most, axis=0, keepdims=True), longest.shape)
    longest[...] = jnp.maximum(most, longest_in[...])
    totals[:n_sums] = own_in[...]
    totals[n_sums:] = twin_in[...]
    to_scalars.wait()

    def add(wanted, whose, source, t, code, msg, place):
        @pl.when(wanted)
        def _():
            block = msg[pl.ds(pl.multiple_of(place * BS, BS), BS), :]
            target = whose * n_sums + (t >> 2) * SC + (code & 3)
            totals[target] += jnp.dot(a_all[source, t], block, preferred_element_type=jnp.float32)

    for n, shift in enumerate(shifts):
        source = lax.rem(me + (NZ - shift), NZ)
        group = groups[shift]

        def step(t, count, n=n, source=source, group=group):
            code = scalars[n, t]
            hit = code >= 0
            place = count >> 1
            whose = (t >> 4) ^ core
            for (lo, size), msg in zip(parts, group):
                here = hit & ((count & 1) == core) & (place >= lo) & (place < lo + size)
                add(here, whose, source, t & (PAIR - 1), code, msg, place - lo)
            return count + hit.astype(jnp.int32)

        def own_step(t, count, n=n, source=source, group=group):
            code = scalars[n, core * PAIR + t]
            hit = code >= 0
            add(hit, 0, source, t, code, group[0], count)
            return count + hit.astype(jnp.int32)

        if shift:
            lax.fori_loop(0, 2 * PAIR, step, jnp.int32(0))
        else:
            lax.fori_loop(0, PAIR, own_step, jnp.int32(0))
    own_out[...] = totals[:n_sums]
    twin_out[...] = totals[n_sums:]


def consume(a_all, sums, longest, shifts, parts, msgs):
    vmem = pl.BlockSpec(memory_space=pltpu.VMEM)
    return pl.pallas_call(
        functools.partial(consume_kernel, shifts, parts),
        out_shape=(
            jax.ShapeDtypeStruct((ROWS * SC, BS, BS), jnp.float32),
            jax.ShapeDtypeStruct((ROWS * SC, BS, BS), jnp.float32),
            jax.ShapeDtypeStruct((8, LANES), jnp.int32),
        ),
        in_specs=[vmem] * (4 + len(msgs)),
        out_specs=(vmem, vmem, vmem),
        scratch_shapes=[
            pltpu.VMEM((2 * ROWS * SC, BS, BS), jnp.float32),
            pltpu.VMEM((NZ, LANES), jnp.int32),
            pltpu.SMEM((NZ, LANES), jnp.int32),
            pltpu.SemaphoreType.DMA,
        ],
        compiler_params=pltpu.CompilerParams(vmem_limit_bytes=28 * 2**20),
        cost_estimate=pl.CostEstimate(flops=2 * BS**3 * 40, bytes_accessed=8 * 2**20, transcendentals=0),
        name="consume",
    )(a_all, *sums, longest, *msgs)


def body(a_blocks, a_index, a_count, b_blocks, b_rows, b_cols, b_count, c_cols, c_count):
    rep = lax.axis_index("rep")
    a_all = lax.dynamic_slice_in_dim(a_blocks, rep * ROWS, ROWS, 0).reshape(PAIR, BS, BS)
    a_all = lax.all_gather(a_all, COL)

    slots_b = jnp.arange(MB, dtype=jnp.int32)
    own = jnp.stack([jnp.where(slots_b < b_count[0, 0], b_rows[0, 0], -1), b_cols[0, 0]])
    slots_a = jnp.arange(SA, dtype=jnp.int32)
    a_meta = jnp.where(slots_a < a_count[:, :, None], a_index, -2)
    slots_c = jnp.arange(SC, dtype=jnp.int32)
    c_meta = jnp.where(slots_c < c_count[:, :, None], c_cols, -1)
    b_own = b_blocks[0, 0]

    blocks = [b_own, along_y(b_own, 1, 0), swap(b_own), along_y(b_own, -1, 1)]
    lists = [own, along_y(own, 1, 0), along_y(own, -1, 1)]

    meta = jnp.concatenate([a_meta.reshape(2 * PAIR), c_meta.reshape(2 * ROWS * SC), own.reshape(2 * MB)])
    meta = jnp.broadcast_to(meta[None, :], (NZ * NX * NCORE, LANES))
    meta = lax.all_to_all(meta, ("z", "x", "core"), 0, 0).reshape(NZ, NX * NCORE, LANES)

    def send(shifts, lo, size):
        outs = pack(meta, lists, blocks, shifts, lo, size)
        return [shift_z(out, shift) for out, shift in zip(outs, shifts)]

    def finish(own_sums, twin_sums):
        return (own_sums + twin_sums).astype(jnp.bfloat16)

    first = (0, CAP)
    msgs = send(SHIFTS[1:FAR], *first)
    near = send(SHIFTS[FAR:] + SHIFTS[:1], *first)
    msgs = near[-1:] + msgs + near[:-1]
    zero = [jnp.zeros((ROWS * SC, BS, BS), jnp.float32)] * 2
    longest = jnp.zeros((8, LANES), jnp.int32)
    *sums, longest = consume(a_all, zero, longest, SHIFTS[:EARLY], [first], msgs[:EARLY])
    *sums, longest = consume(a_all, sums, longest, SHIFTS[EARLY:], [first], msgs[EARLY:])

    def again(*_):
        rest = (CAP, PAIR - CAP)
        both = msgs[:1] + [m for pair in zip(msgs[1:], send(SHIFTS[1:], *rest)) for m in pair]
        own_sums, twin_sums, _ = consume(a_all, zero, longest, SHIFTS, [first, rest], both)
        return finish(own_sums, swap(twin_sums))

    out = lax.cond(longest[0, 0] > 2 * CAP, again, finish, sums[0], swap(sums[1]))
    return out.reshape(ROWS, 1, SC, BS, BS)


def solution(mesh):
    fine = Mesh(mesh.devices.reshape(NZ, NYL, NX, NCORE, NREP), AXES)
    row = ("z", "yl")
    return jax.shard_map(
        body,
        mesh=fine,
        in_specs=tuple(
            P(row, COL, *([None] * (rank - 2))) for rank in (5, 3, 2, 5, 3, 3, 2, 3, 2)
        ),
        out_specs=P(("z", "yl", "rep"), COL, None, None, None),
        check_vma=False,
    )
```

```python
import functools

import jax
import jax.numpy as jnp
from jax import lax
from jax.experimental import pallas as pl
from jax.experimental.pallas import tpu as pltpu
from jax.sharding import Mesh
from jax.sharding import PartitionSpec as P

NZ, NYL, NX, NCORE, NREP = 8, 2, 4, 2, 2
AXES = ("z", "yl", "x", "core", "rep")
COL = ("x", "core")
BS, SA, SC, MB = 128, 2, 4, 32
ROWS = 4
PAIR = ROWS * 2 * SA
CAP = 8
HDR = 16
LANES = 128
SHIFTS = (0, 4, 3, -3, 2, -2, 1, -1)
WIDE = 256
FAR = 5
EARLY = 4


def along_y(value, steps, other_core):
    n = NYL * NREP
    pairs = []
    for y in range(n):
        for core in range(NCORE):
            ends = []
            for where, at in ((y, core), ((y + steps) % n, core ^ other_core)):
                ends.append(((where % NYL) * NCORE + at) * NREP + where // NYL)
            pairs.append(tuple(ends))
    return lax.ppermute(value, ("yl", "core", "rep"), pairs)


def shift_z(value, steps):
    if steps == 0:
        return value
    return lax.ppermute(value, "z", [(z, (z + steps) % NZ) for z in range(NZ)])


def swap(value):
    return lax.ppermute(value, "core", [(0, 1), (1, 0)])


def find_codes(wanted, columns, own, other, is_own, lane):
    slot = jnp.zeros((NZ, LANES), jnp.int32)
    target = jnp.full((NZ, LANES), -5, jnp.int32)
    for m in range(MB):
        hit = wanted == jnp.where(is_own, own[0, m], other[0, m])
        slot = jnp.where(hit, m, slot)
        target = jnp.where(hit, jnp.where(is_own, own[1, m], other[1, m]), target)
    moved = {d: pltpu.roll(columns, d % LANES, 1) if d else columns for d in range(1 - SC, SC)}
    code = jnp.full((NZ, LANES), -1, jnp.int32)
    for s in range(SC):
        column = moved[-s]
        for o in range(1, SC):
            column = jnp.where((lane & (SC - 1)) == o, moved[o - s], column)
        code = jnp.where(column == target, slot * SC + s, code)
    return code


def pack_kernel(shifts, lo, size, meta, own, other, twin_other, *rest):
    lists, outs = rest[:4], rest[4 : 4 + len(shifts)]
    held, codes, scalars, sems = rest[4 + len(shifts) :]
    core = lax.axis_index("core")
    mine, twins = core * 2 * MB, (1 - core) * 2 * MB
    copies = []
    for n, (source, first) in enumerate(zip(lists, (mine, mine + MB, twins, twins + MB))):
        copies.append(pltpu.make_async_copy(source, held.at[pl.ds(first, MB)], sems.at[n]))
        copies[-1].start()
    yl = lax.axis_index("yl")
    me = lax.axis_index("z")
    x = lax.axis_index("x")
    lane = lax.broadcasted_iota(jnp.int32, (NZ, LANES), 1)
    is_own = ((lane >> 1) & 1) == yl
    first_half = lax.axis_index("rep") == 0

    def pick(col, start, length):
        rows = jnp.concatenate([meta[z, pl.ds(col, 1), :] for z in range(NZ)], axis=0)
        low = pltpu.roll(rows, LANES - start, 1) if start else rows
        return jnp.where(first_half, low, pltpu.roll(rows, LANES - start - length, 1))

    wanted = jnp.where(lane < PAIR, pick(me, 0, PAIR), -2)
    def as_list(row, start):
        return {
            (n, m): row[:, start + n * MB + m : start + n * MB + m + 1] for n in range(2) for m in range(MB)
        }

    twin_own = as_list(meta[me, pl.ds(x * NCORE + 1 - core, 1), :], 4 * PAIR)
    other, twin_other = as_list(other[0:1, :], 0), as_list(twin_other[0:1, :], 0)
    code = find_codes(wanted, pick(x * NCORE + core, 2 * PAIR, ROWS * SC), own, other, is_own, lane)
    twin = find_codes(wanted, pick(x * NCORE + 1 - core, 2 * PAIR, ROWS * SC), twin_own, twin_other, is_own, lane)
    code, twin = jnp.where(core == 0, code, twin), jnp.where(core == 0, twin, code)
    code = jnp.where(lane < PAIR, code, jnp.where(lane < 2 * PAIR, pltpu.roll(twin, PAIR, 1), -1))
    codes[...] = code
    to_scalars = pltpu.make_async_copy(codes, scalars, sems.at[4])
    to_scalars.start()
    head = jnp.concatenate([code, jnp.full((HDR - NZ, LANES), -1, jnp.int32)], axis=0)
    head = head.astype(jnp.float32).astype(jnp.bfloat16)
    for out, shift in zip(outs, shifts):
        out[pl.ds((size if shift else PAIR) * BS, HDR), :] = head
    to_scalars.wait()
    for copy in copies:
        copy.wait()

    def block(t, code):
        return (t >> 4) * (2 * MB) + jnp.where(((t >> 1) & 1) == yl, 0, MB) + (code >> 2)

    for out, shift in zip(outs, shifts):
        z = lax.rem(me + (NZ + shift), NZ)

        def step(t, count, out=out, z=z):
            code = scalars[z, t]
            hit = code >= 0
            place = count >> 1

            @pl.when(hit & ((count & 1) == core) & (place >= lo) & (place < lo + size))
            def _():
                out[pl.ds(pl.multiple_of((place - lo) * BS, BS), BS), :] = held[block(t, code)]

            return count + hit.astype(jnp.int32)

        def steps(n, count, step=step):
            for k in range(8):
                count = step(n * 8 + k, count)
            return count

        def own_step(t, count, out=out, z=z):
            t = core * PAIR + t
            code = scalars[z, t]
            hit = code >= 0

            @pl.when(hit)
            def _():
                out[pl.ds(pl.multiple_of(count * BS, BS), BS), :] = held[block(t, code)]

            return count + hit.astype(jnp.int32)

        if shift:
            lax.fori_loop(0, 2 * PAIR // 8, steps, jnp.int32(0))
        else:
            lax.fori_loop(0, PAIR, own_step, jnp.int32(0))


def pack(meta, lists, blocks, shifts, lo, size):
    smem, vmem, hbm = (pl.BlockSpec(memory_space=m) for m in (pltpu.SMEM, pltpu.VMEM, pl.ANY))
    return pl.pallas_call(
        functools.partial(pack_kernel, shifts, lo, size),
        out_shape=[
            jax.ShapeDtypeStruct(((size if shift else PAIR) * BS + HDR, BS), jnp.bfloat16)
            for shift in shifts
        ],
        in_specs=[vmem, smem, vmem, vmem] + [hbm] * 4,
        out_specs=[vmem] * len(shifts),
        scratch_shapes=[
            pltpu.VMEM((4 * MB, BS, BS), jnp.bfloat16),
            pltpu.VMEM((NZ, LANES), jnp.int32),
            pltpu.SMEM((NZ, LANES), jnp.int32),
            pltpu.SemaphoreType.DMA((5,)),
        ],
        compiler_params=pltpu.CompilerParams(vmem_limit_bytes=28 * 2**20),
        name="pack",
    )(meta, *lists, *blocks)


def consume_kernel(shifts, parts, a_all, own_in, twin_in, longest_in, *rest):
    width = {shift: len(parts) if shift else 1 for shift in shifts}
    count_msgs = sum(width.values())
    msgs, (own_out, twin_out, longest, totals, codes, scalars, sem) = rest[:count_msgs], rest[count_msgs:]
    n_sums = ROWS * SC
    groups = {}
    for shift in shifts:
        groups[shift], msgs = msgs[: width[shift]], msgs[width[shift] :]
    me = lax.axis_index("z")
    core = lax.axis_index("core")
    row = lax.broadcasted_iota(jnp.int32, (HDR, LANES), 0)
    most = jnp.zeros((HDR, 1), jnp.int32)
    for n, shift in enumerate(shifts):
        source = lax.rem(me + (NZ - shift), NZ)
        head = groups[shift][0][pl.ds((parts[0][1] if shift else PAIR) * BS, HDR), :]
        head = head.astype(jnp.float32).astype(jnp.int32)
        codes[pl.ds(n, 1), :] = jnp.sum(jnp.where(row == me, head, 0), axis=0, keepdims=True)
        sent = (head >= 0) & (row != source)
        most = jnp.maximum(most, jnp.sum(sent.astype(jnp.int32), axis=1, keepdims=True))
    to_scalars = pltpu.make_async_copy(codes, scalars, sem)
    to_scalars.start()
    most = jnp.broadcast_to(jnp.max(most, axis=0, keepdims=True), longest.shape)
    longest[...] = jnp.maximum(most, longest_in[...])
    totals[:n_sums] = own_in[...]
    totals[n_sums:] = twin_in[...]
    to_scalars.wait()

    def add(wanted, whose, source, t, code, msg, place):
        @pl.when(wanted)
        def _():
            block = msg[pl.ds(pl.multiple_of(place * BS, BS), BS), :]
            target = whose * n_sums + (t >> 2) * SC + (code & 3)
            totals[target] += jnp.dot(a_all[source, t], block, preferred_element_type=jnp.float32)

    for n, shift in enumerate(shifts):
        source = lax.rem(me + (NZ - shift), NZ)
        group = groups[shift]

        def step(t, count, n=n, source=source, group=group):
            code = scalars[n, t]
            hit = code >= 0
            place = count >> 1
            whose = (t >> 4) ^ core
            for (lo, size), msg in zip(parts, group):
                here = hit & ((count & 1) == core) & (place >= lo) & (place < lo + size)
                add(here, whose, source, t & (PAIR - 1), code, msg, place - lo)
            return count + hit.astype(jnp.int32)

        def own_step(t, count, n=n, source=source, group=group):
            code = scalars[n, core * PAIR + t]
            hit = code >= 0
            add(hit, 0, source, t, code, group[0], count)
            return count + hit.astype(jnp.int32)

        if shift:
            lax.fori_loop(0, 2 * PAIR, step, jnp.int32(0))
        else:
            lax.fori_loop(0, PAIR, own_step, jnp.int32(0))
    own_out[...] = totals[:n_sums]
    twin_out[...] = totals[n_sums:]


def consume(a_all, sums, longest, shifts, parts, msgs):
    vmem = pl.BlockSpec(memory_space=pltpu.VMEM)
    return pl.pallas_call(
        functools.partial(consume_kernel, shifts, parts),
        out_shape=(
            jax.ShapeDtypeStruct((ROWS * SC, BS, BS), jnp.float32),
            jax.ShapeDtypeStruct((ROWS * SC, BS, BS), jnp.float32),
            jax.ShapeDtypeStruct((8, LANES), jnp.int32),
        ),
        in_specs=[vmem] * (4 + len(msgs)),
        out_specs=(vmem, vmem, vmem),
        scratch_shapes=[
            pltpu.VMEM((2 * ROWS * SC, BS, BS), jnp.float32),
            pltpu.VMEM((NZ, LANES), jnp.int32),
            pltpu.SMEM((NZ, LANES), jnp.int32),
            pltpu.SemaphoreType.DMA,
        ],
        compiler_params=pltpu.CompilerParams(vmem_limit_bytes=28 * 2**20),
        cost_estimate=pl.CostEstimate(flops=2 * BS**3 * 40, bytes_accessed=8 * 2**20, transcendentals=0),
        name="consume",
    )(a_all, *sums, longest, *msgs)


def body(a_blocks, a_index, a_count, b_blocks, b_rows, b_cols, b_count, c_cols, c_count):
    rep = lax.axis_index("rep")
    a_all = lax.dynamic_slice_in_dim(a_blocks, rep * ROWS, ROWS, 0).reshape(PAIR, BS, BS)
    a_all = lax.all_gather(a_all, COL)

    slots_b = jnp.arange(MB, dtype=jnp.int32)
    own = jnp.stack([jnp.where(slots_b < b_count[0, 0], b_rows[0, 0], -1), b_cols[0, 0]])
    slots_a = jnp.arange(SA, dtype=jnp.int32)
    a_meta = jnp.where(slots_a < a_count[:, :, None], a_index, -2)
    slots_c = jnp.arange(SC, dtype=jnp.int32)
    c_meta = jnp.where(slots_c < c_count[:, :, None], c_cols, -1)
    b_own = b_blocks[0, 0]

    blocks = [b_own, along_y(b_own, 1, 0), swap(b_own), along_y(b_own, -1, 1)]
    wide = jnp.broadcast_to(jnp.pad(own.reshape(1, 2 * MB), ((0, 0), (0, LANES - 2 * MB))), (WIDE, LANES))
    lists = [own, along_y(wide, 1, 0), along_y(wide, -1, 1)]

    meta = jnp.concatenate([a_meta.reshape(2 * PAIR), c_meta.reshape(2 * ROWS * SC), own.reshape(2 * MB)])
    meta = jnp.broadcast_to(meta[None, :], (NZ * NX * NCORE, LANES))
    meta = lax.all_to_all(meta, ("z", "x", "core"), 0, 0).reshape(NZ, NX * NCORE, LANES)

    def send(shifts, lo, size):
        outs = pack(meta, lists, blocks, shifts, lo, size)
        return [shift_z(out, shift) for out, shift in zip(outs, shifts)]

    def finish(own_sums, twin_sums):
        return (own_sums + twin_sums).astype(jnp.bfloat16)

    first = (0, CAP)
    msgs = send(SHIFTS[1:FAR], *first)
    near = send(SHIFTS[FAR:] + SHIFTS[:1], *first)
    msgs = near[-1:] + msgs + near[:-1]
    zero = [jnp.zeros((ROWS * SC, BS, BS), jnp.float32)] * 2
    longest = jnp.zeros((8, LANES), jnp.int32)
    *sums, longest = consume(a_all, zero, longest, SHIFTS[:EARLY], [first], msgs[:EARLY])
    *sums, longest = consume(a_all, sums, longest, SHIFTS[EARLY:], [first], msgs[EARLY:])

    def again(*_):
        rest = (CAP, PAIR - CAP)
        both = msgs[:1] + [m for pair in zip(msgs[1:], send(SHIFTS[1:], *rest)) for m in pair]
        own_sums, twin_sums, _ = consume(a_all, zero, longest, SHIFTS, [first, rest], both)
        return finish(own_sums, swap(twin_sums))

    out = lax.cond(longest[0, 0] > 2 * CAP, again, finish, sums[0], swap(sums[1]))
    return out.reshape(ROWS, 1, SC, BS, BS)


def solution(mesh):
    fine = Mesh(mesh.devices.reshape(NZ, NYL, NX, NCORE, NREP), AXES)
    row = ("z", "yl")
    return jax.shard_map(
        body,
        mesh=fine,
        in_specs=tuple(
            P(row, COL, *([None] * (rank - 2))) for rank in (5, 3, 2, 5, 3, 3, 2, 3, 2)
        ),
        out_specs=P(("z", "yl", "rep"), COL, None, None, None),
        check_vma=False,
    )
```
